512 devices in a mesh: patch: 32 (over y_lo, z), head: 16 (over y_hi, x, core).
Axes of the slice: x: 4, y: 4 (y_hi: 2, y_lo: 2; y = y_hi * 2 + y_lo), z: 16, core: 2. Of those that a mesh axis runs over, the one named last changes fastest.
Arguments:
- queries: bfloat16 [3072, 8192], P('head', 'patch'), may hold values from -8 to 8
- fresh_kv: bfloat16 [8192, 48, 128], P('patch', 'head'), may hold values from -8 to 8
- stale_kv: bfloat16 [8192, 48, 128], P('patch', 'head'), may hold values from -8 to 8
- residual: bfloat16 [3072, 8192], P('head', 'patch'), may hold values from -6 to 6
- gate: float32 [3072], P('head'), may hold values from 0.5 to 2
- w_out: bfloat16 [3072, 3072], P('head'), may hold values from -0.109375 to 0.109375
Outputs:
- block_out: bfloat16 [3072, 8192], P('head', 'patch')
The draws below stay inside these ranges and needn't reach their ends.
All inputs are finite; a program needn't handle non-finite values.
Results may differ from the reference program's by a relative error of at most 0.0065.
Values may be sent and summed in bfloat16 or wider, within the bound.
A program may use at most 64 MiB of HBM per device.

```python
import math
import jax
import jax.numpy as jnp
from jax import lax

D = 3072
HEADS = 48
HD = 64
TOK_DEV = 256
TOKENS = 8192
N_PATCH = 32


def draw_queries(key, part):
    own_key = jax.random.fold_in(key, 1)
    base = 1.7 * jnp.clip(jax.random.normal(own_key, (TOKENS, HEADS, HD)), -4.5, 4.5)
    return base.reshape(TOKENS, HEADS * HD).T.astype(jnp.bfloat16)


def draw_stale_kv(key, part):
    own_key = jax.random.fold_in(key, 2)
    value_key = jax.random.fold_in(own_key, 5)
    key_part = 1.7 * jnp.clip(jax.random.normal(own_key, (TOKENS, HEADS, HD)), -4.5, 4.5)
    values = 1.7 * jnp.clip(jax.random.normal(value_key, (TOKENS, HEADS, HD)), -4.5, 4.5)
    return jnp.concatenate([key_part, values], axis=2).astype(jnp.bfloat16)


def levels(stream_key, dims, pieces, low, top_value):
    factor_of = 1.0
    for dim, shards_of in pieces:
        draws = jax.random.uniform(jax.random.fold_in(jax.random.fold_in(stream_key, 6), dim), (shards_of,), jnp.float32, low / len(pieces), top_value / len(pieces))
        factor_of = factor_of * jnp.repeat(jnp.exp(draws), dims[dim] // shards_of).reshape((-1,) + (1,) * (len(dims) - 1 - dim))
    return factor_of


def centred(rng, shape, spread, limit, shards=(), held_as=jnp.bfloat16):
    drawn = jax.random.normal(rng, shape, jnp.float32) * spread
    if len(shards) > 0:
        drawn = levels(rng, shape, shards, -0.22, 0.18) * drawn
    return jnp.clip(drawn, min=-limit, max=limit).astype(held_as)


def setup_inputs(seed: int = 0) -> dict:
    seeds = jax.random.split(jax.random.key(seed), 7)
    queries = draw_queries(jax.random.fold_in(seeds[6], 71), 0)
    fresh_kv = centred(seeds[1], (TOKENS, HEADS, 2 * HD), 1.7, 8.0, ((0, 32), (1, 16)))
    stale_kv = draw_stale_kv(jax.random.fold_in(seeds[6], 71), 0)
    residual = centred(seeds[3], (D, TOKENS), 1.0, 6.0, ((0, 16), (1, 32)))
    gate = jnp.clip(0.5 + 1.5 * jax.random.uniform(seeds[4], (D,), jnp.float32) ** levels(seeds[4], (D,), ((0, 16),), -0.2, 0.2), 0.5, 2.0)
    w_out = centred(seeds[5], (D, HEADS * HD), (HEADS * HD) ** -0.5, 0.109375, ((0, 16),))
    return {"queries": queries, "fresh_kv": fresh_kv, "stale_kv": stale_kv, "residual": residual, "gate": gate, "w_out": w_out}


def reference(queries, fresh_kv, stale_kv, residual, gate, w_out):
    score_scale = 1.0 / math.sqrt(HD)

    def one_patch(patch_id):
        offset = (patch_id * TOK_DEV).astype(jnp.int32)
        fresh_rows = lax.dynamic_slice_in_dim(fresh_kv, offset, TOK_DEV, 0)
        zero = jnp.zeros((), jnp.int32)
        merged = lax.dynamic_update_slice(stale_kv, fresh_rows, (offset, zero, zero))
        query_part = lax.dynamic_slice_in_dim(queries, offset, TOK_DEV, 1)
        query_part = query_part.reshape(HEADS, HD, TOK_DEV).astype(jnp.float32)
        key_part = merged[:, :, :HD].astype(jnp.float32)
        value_part = merged[:, :, HD:].astype(jnp.float32)
        scores = jnp.einsum('hdi,jhd->hij', query_part, key_part) * score_scale
        row_top = lax.optimization_barrier(jnp.max(scores, axis=2, keepdims=True))
        weights_exp = jnp.exp(scores - row_top)
        probs = lax.optimization_barrier(weights_exp.astype(jnp.bfloat16)).astype(jnp.float32)
        numerator = jnp.einsum('hij,jhd->hdi', probs, value_part)
        denominator = lax.optimization_barrier(jnp.sum(weights_exp, axis=2))
        attended = (numerator / denominator[:, None, :]).astype(jnp.bfloat16)
        return attended.reshape(HEADS * HD, TOK_DEV)
    blocks = lax.map(one_patch, jnp.arange(N_PATCH, dtype=jnp.int32))
    attended = jnp.transpose(blocks, (1, 0, 2)).reshape(HEADS * HD, TOKENS)
    projected = jnp.dot(w_out, attended, preferred_element_type=jnp.float32)
    result = residual.astype(jnp.float32) + gate.astype(jnp.float32)[:, None] * projected
    return result.astype(jnp.bfloat16)
```

```python
import functools
import math

import jax
import jax.numpy as jnp
from jax import lax
from jax.experimental import pallas as pl
from jax.experimental.pallas import tpu as pltpu
from jax.sharding import PartitionSpec as P

MESH = pl.DeviceIdType.MESH
HEADS = 3
HD = 64
TOK = 256
RING = 16
LOG2E = 1.4426950408889634
HALF = TOK // 2
ROWS = HD + 16


def fused(q_in, fresh_in, stale_in, w_in, out, kv, fresh, qb, qx, wb, wp, qs, acc, top,
          opart, ostat, oin, ostat_in, att, load_sem, z_send, z_recv, y_send, y_recv,
          g_send, g_recv, c_send, c_recv):
    patch = lax.axis_index("patch")
    head = lax.axis_index("head")
    y_lo, z = patch // RING, patch % RING
    y_hi, x, core = head // 8, (head // 2) % 4, head % 2
    right = (y_lo * RING + (z + 1) % RING, head)
    left = (y_lo * RING + (z + RING - 1) % RING, head)
    across = ((1 - y_lo) * RING + z, head)
    sibling = (patch, head + 1 - 2 * core)

    def plane(j):
        return (patch, ((y_hi + j // 4) % 2) * 8 + ((x + j % 4) % 4) * 2 + core)

    def plane_back(j):
        return ((y_hi + j // 4) % 2) * 8 + ((x + 4 - j % 4) % 4) * 2 + core

    loads = [
        pltpu.make_async_copy(stale_in, kv.at[:, 0], load_sem.at[0]),
        pltpu.make_async_copy(q_in, qb, load_sem.at[1]),
        pltpu.make_async_copy(fresh_in, fresh, load_sem.at[2]),
        pltpu.make_async_copy(w_in, wb, load_sem.at[3]),
    ]
    for load in loads:
        load.start()

    barrier = pltpu.get_barrier_semaphore()
    partners = [right, left, across, sibling] + [plane(j) for j in range(1, 8)]
    for partner in partners:
        pl.semaphore_signal(barrier, inc=1, device_id=partner, device_id_type=MESH)
    pl.semaphore_wait(barrier, len(partners))

    def remote(src, dst, send, recv, device):
        return pltpu.make_async_remote_copy(
            src_ref=src, dst_ref=dst, send_sem=send, recv_sem=recv,
            device_id=device, device_id_type=MESH)

    def hop_right(h, s, rows=slice(None)):
        return remote(kv.at[h, s, rows], kv.at[h, s + 1, rows], z_send.at[0, h, s],
                      z_recv.at[0, h, s], right)

    def hop_left(h, s, rows=slice(None)):
        return remote(kv.at[h, (RING - s) % RING, rows], kv.at[h, RING - 1 - s, rows],
                      z_send.at[1, h, s], z_recv.at[1, h, s], left)

    low, high = pl.ds(0, HALF), pl.ds(HALF, HALF)

    loads[0].wait()
    for h in range(HEADS):
        hop_right(h, 0).start()
        hop_left(h, 0).start()
    loads[1].wait()
    q_move = remote(qb, qx, y_send.at[0], y_recv.at[0], across)
    q_move.start()

    lane = lax.broadcasted_iota(jnp.int32, (1, 2 * HD), 1)

    def with_ones(block):
        swapped = jnp.where(lane < HD, jnp.ones_like(block), block)
        return swapped.T[HD - 16:]

    def first(h, block, lo):
        cols = pl.ds(lo, TOK)
        scores = jnp.dot(block, qs[h, :, cols], preferred_element_type=jnp.float32)
        high_score = jnp.max(scores, axis=0, keepdims=True)
        weights = jnp.exp2((scores - high_score) * LOG2E).astype(jnp.bfloat16)
        acc[h, :, cols] = jnp.dot(with_ones(block), weights, preferred_element_type=jnp.float32)
        top[h, :, cols] = high_score

    def update(h, block, lo, width):
        cols = pl.ds(lo, width)
        scores = jnp.dot(block, qs[h, :, cols], preferred_element_type=jnp.float32)
        old = top[h, :, cols]
        new = jnp.maximum(old, jnp.max(scores, axis=0, keepdims=True))
        weights = jnp.exp2((scores - new) * LOG2E).astype(jnp.bfloat16)
        part = jnp.dot(with_ones(block), weights, preferred_element_type=jnp.float32)
        acc[h, :, cols] = acc[h, :, cols] * jnp.exp2((old - new) * LOG2E) + part
        top[h, :, cols] = new

    def place_queries(src, lo):
        for h in range(HEADS):
            scaled = src[pl.ds(h * HD, HD), :] * jnp.bfloat16(1.0 / math.sqrt(HD))
            qs[h, pl.ds(0, HD), pl.ds(lo, TOK)] = scaled
            qs[h, pl.ds(HD, HD), pl.ds(lo, TOK)] = jnp.zeros((HD, TOK), jnp.bfloat16)

    place_queries(qb, 0)
    loads[2].wait()

    def own_fresh(h, carry):
        first(h, fresh[h], 0)
        return carry

    lax.fori_loop(0, HEADS, own_fresh, 0)

    loads[3].wait()
    for h in range(HEADS):
        for k in range(8):
            pair = [wb[:, pl.ds((2 * k + e) * HEADS * HD + h * HD, HD)] for e in range(2)]
            wp[h, :, pl.ds(k * 128, 128)] = jnp.concatenate(pair, axis=1)

    q_move.wait_recv()
    place_queries(qx, TOK)

    def own_stale(h, carry):
        first(h, kv[h, 0], TOK)
        return carry

    lax.fori_loop(0, HEADS, own_stale, 0)

    def ring_step(t, carry):
        s, h = 1 + t // HEADS, t % HEADS
        hop_right(h, s - 1).wait_recv()

        @pl.when(s < 7)
        def _():
            hop_right(h, s).start()

        @pl.when(s == 7)
        def _():
            hop_right(h, s, low).start()

        hop_left(h, s - 1).wait_recv()

        @pl.when(s < 7)
        def _():
            hop_left(h, s).start()

        @pl.when(s == 7)
        def _():
            hop_left(h, s, high).start()

        update(h, kv[h, s], 0, 2 * TOK)
        update(h, kv[h, RING - s], 0, 2 * TOK)
        return carry

    lax.fori_loop(0, 7 * HEADS, ring_step, 0)

    def o_moves(h):
        return (remote(opart.at[h], oin.at[h], y_send.at[1 + h], y_recv.at[1 + h], across),
                remote(ostat.at[h], ostat_in.at[h], y_send.at[4 + h], y_recv.at[4 + h], across))

    def last_step(h, carry):
        hop_right(h, 7, low).wait_recv()
        hop_left(h, 7, high).wait_recv()
        block = kv[h, 8]
        update(h, block, TOK, TOK)
        cols = pl.ds(TOK, TOK)
        total = acc[h, pl.ds(0, 8), cols][0:1]
        opart[h] = (acc[h, pl.ds(16, HD), cols] / total).astype(jnp.bfloat16)
        ostat[h, pl.ds(0, 1)] = top[h, :, cols]
        ostat[h, pl.ds(1, 1)] = total
        for move in o_moves(h):
            move.start()
        update(h, block, 0, TOK)
        return carry

    ostat[...] = jnp.zeros_like(ostat)
    lax.fori_loop(0, HEADS, last_step, 0)

    def sent(t, carry):
        s, h = t // HEADS, t % HEADS
        hop_right(h, s).wait_send()
        hop_left(h, s).wait_send()
        return carry

    lax.fori_loop(0, 7 * HEADS, sent, 0)
    for h in range(HEADS):
        hop_right(h, 7, low).wait_send()
        hop_left(h, 7, high).wait_send()
    q_move.wait_send()

    def g_move(h, j):
        return remote(att.at[h, head], att.at[h, head], g_send.at[h, j], g_recv.at[h, j], plane(j))

    def c_move(h, j):
        slot = plane_back(j)
        return remote(att.at[h, slot], att.at[h, slot], c_send.at[h, j], c_recv.at[h, j], sibling)

    def combine(h, carry):
        for move in o_moves(h):
            move.wait_recv()
        cols = pl.ds(0, TOK)
        top_a, top_b = top[h, :, cols], ostat_in[h, pl.ds(0, 1)]
        new = jnp.maximum(top_a, top_b)
        scale_a = jnp.exp2((top_a - new) * LOG2E)
        total_a = acc[h, pl.ds(0, 8), cols][0:1] * scale_a
        total_b = ostat_in[h, pl.ds(1, 1)] * jnp.exp2((top_b - new) * LOG2E)
        inverse = 1.0 / (total_a + total_b)
        mixed = (acc[h, pl.ds(16, HD), cols] * (scale_a * inverse)
                 + oin[h].astype(jnp.float32) * (total_b * inverse))
        att[h, head] = mixed.astype(jnp.bfloat16)
        for j in (6, 5, 7, 4, 2, 1, 3):
            g_move(h, j).start()
        c_move(h, 0).start()
        return carry

    lax.fori_loop(0, HEADS, combine, 0)

    def project(h, carry):
        for j in (1, 3, 2, 4, 5, 7, 6):
            g_move(h, j).wait_recv()
            c_move(h, j).start()
        for j in range(8):
            c_move(h, j).wait_recv()
        part = jnp.dot(wp[h], att[h].reshape(16 * HD, TOK), preferred_element_type=jnp.float32)
        out[...] = out[...] + part
        return carry

    out[...] = jnp.zeros_like(out)
    lax.fori_loop(0, HEADS, project, 0)

    def drain(h, carry):
        for move in o_moves(h):
            move.wait_send()
        for j in range(1, 8):
            g_move(h, j).wait_send()
        for j in range(8):
            c_move(h, j).wait_send()
        return carry

    lax.fori_loop(0, HEADS, drain, 0)


def on_device(queries, fresh_kv, stale_kv, residual, gate, w_out):
    bf16, f32 = jnp.bfloat16, jnp.float32
    any_space = pl.BlockSpec(memory_space=pl.ANY)
    dma = pltpu.SemaphoreType.DMA
    projected = pl.pallas_call(
        fused,
        out_shape=jax.ShapeDtypeStruct((HEADS * HD, TOK), f32),
        in_specs=[any_space] * 4,
        out_specs=pl.BlockSpec(memory_space=pltpu.VMEM),
        scratch_shapes=[
            pltpu.VMEM((HEADS, RING, TOK, 2 * HD), bf16),
            pltpu.VMEM((HEADS, TOK, 2 * HD), bf16),
            pltpu.VMEM((HEADS * HD, TOK), bf16),
            pltpu.VMEM((HEADS * HD, TOK), bf16),
            pltpu.VMEM((HEADS * HD, 16 * HEADS * HD), bf16),
            pltpu.VMEM((HEADS, HEADS * HD, 16 * HD), bf16),
            pltpu.VMEM((HEADS, 2 * HD, 2 * TOK), bf16),
            pltpu.VMEM((HEADS, ROWS, 2 * TOK), f32),
            pltpu.VMEM((HEADS, 1, 2 * TOK), f32),
            pltpu.VMEM((HEADS, HD, TOK), bf16),
            pltpu.VMEM((HEADS, 8, TOK), f32),
            pltpu.VMEM((HEADS, HD, TOK), bf16),
            pltpu.VMEM((HEADS, 8, TOK), f32),
            pltpu.VMEM((HEADS, 16, HD, TOK), bf16),
            dma((4,)),
            dma((2, HEADS, 8)),
            dma((2, HEADS, 8)),
            dma((7,)),
            dma((7,)),
            dma((HEADS, 8)),
            dma((HEADS, 8)),
            dma((HEADS, 8)),
            dma((HEADS, 8)),
        ],
        compiler_params=pltpu.CompilerParams(
            collective_id=0, has_side_effects=True, vmem_limit_bytes=40 * 1024 * 1024),
        cost_estimate=pl.CostEstimate(
            flops=2_000_000_000, bytes_accessed=4_000_000, transcendentals=6_500_000),
    )(queries, fresh_kv.transpose(1, 0, 2), stale_kv.transpose(1, 0, 2), w_out)
    result = residual.astype(f32) + gate[:, None] * projected
    return result.astype(bf16)


def solution(mesh):
    placed = (
        P("head", "patch"),
        P("patch", "head", None),
        P("patch", "head", None),
        P("head", "patch"),
        P("head"),
        P("head", None),
    )
    return jax.shard_map(
        on_device, mesh=mesh, in_specs=placed, out_specs=P("head", "patch"), check_vma=False
    )
```

```python
import functools
import math

import jax
import jax.numpy as jnp
from jax import lax
from jax.experimental import pallas as pl
from jax.experimental.pallas import tpu as pltpu
from jax.sharding import PartitionSpec as P

MESH = pl.DeviceIdType.MESH
HEADS = 3
HD = 64
TOK = 256
RING = 16
LOG2E = 1.4426950408889634
HALF = TOK // 2
RIGHT_HOPS, LEFT_HOPS = 7, 8
ROWS = HD + 16


def fused(q_in, fresh_in, stale_in, w_in, out, kv, fresh, qb, qx, wb, wp, qs, acc, top,
          opart, ostat, oin, ostat_in, att, load_sem, z_send, z_recv, y_send, y_recv,
          g_send, g_recv, c_send, c_recv):
    patch = lax.axis_index("patch")
    head = lax.axis_index("head")
    y_lo, z = patch // RING, patch % RING
    y_hi, x, core = head // 8, (head // 2) % 4, head % 2
    right = (y_lo * RING + (z + 1) % RING, head)
    left = (y_lo * RING + (z + RING - 1) % RING, head)
    across = ((1 - y_lo) * RING + z, head)
    sibling = (patch, head + 1 - 2 * core)

    def plane(j):
        return (patch, ((y_hi + j // 4) % 2) * 8 + ((x + j % 4) % 4) * 2 + core)

    def plane_back(j):
        return ((y_hi + j // 4) % 2) * 8 + ((x + 4 - j % 4) % 4) * 2 + core

    loads = [
        pltpu.make_async_copy(stale_in, kv.at[:, 0], load_sem.at[0]),
        pltpu.make_async_copy(q_in, qb, load_sem.at[1]),
        pltpu.make_async_copy(fresh_in, fresh, load_sem.at[2]),
        pltpu.make_async_copy(w_in, wb, load_sem.at[3]),
    ]
    for load in loads:
        load.start()

    barrier = pltpu.get_barrier_semaphore()
    partners = [right, left, across, sibling] + [plane(j) for j in range(1, 8)]
    for partner in partners:
        pl.semaphore_signal(barrier, inc=1, device_id=partner, device_id_type=MESH)
    pl.semaphore_wait(barrier, len(partners))

    def remote(src, dst, send, recv, device):
        return pltpu.make_async_remote_copy(
            src_ref=src, dst_ref=dst, send_sem=send, recv_sem=recv,
            device_id=device, device_id_type=MESH)

    def hop_right(h, part, s):
        rows = pl.ds(part * HALF, HALF)
        return remote(kv.at[h, s, rows], kv.at[h, s + 1, rows], z_send.at[0, h, part, s],
                      z_recv.at[0, h, part, s], right)

    def hop_left(h, part, s):
        rows = pl.ds(part * HALF, HALF)
        return remote(kv.at[h, (RING - s) % RING, rows], kv.at[h, RING - 1 - s, rows],
                      z_send.at[1, h, part, s], z_recv.at[1, h, part, s], left)

    loads[0].wait()
    for h in range(HEADS):
        for part in range(2):
            hop_right(h, part, 0).start()
            hop_left(h, part, 0).start()
    loads[1].wait()
    q_move = remote(qb, qx, y_send.at[0], y_recv.at[0], across)
    q_move.start()

    lane = lax.broadcasted_iota(jnp.int32, (1, 2 * HD), 1)

    def with_ones(block):
        swapped = jnp.where(lane < HD, jnp.ones_like(block), block)
        return swapped.T[HD - 16:]

    def first(h, block, lo):
        cols = pl.ds(lo, TOK)
        scores = jnp.dot(block, qs[h, :, cols], preferred_element_type=jnp.float32)
        high_score = jnp.max(scores, axis=0, keepdims=True)
        weights = jnp.exp2((scores - high_score) * LOG2E).astype(jnp.bfloat16)
        acc[h, :, cols] = jnp.dot(with_ones(block), weights, preferred_element_type=jnp.float32)
        top[h, :, cols] = high_score

    def update(h, block, lo, width):
        cols = pl.ds(lo, width)
        scores = jnp.dot(block, qs[h, :, cols], preferred_element_type=jnp.float32)
        old = top[h, :, cols]
        new = jnp.maximum(old, jnp.max(scores, axis=0, keepdims=True))
        weights = jnp.exp2((scores - new) * LOG2E).astype(jnp.bfloat16)
        part = jnp.dot(with_ones(block), weights, preferred_element_type=jnp.float32)
        acc[h, :, cols] = acc[h, :, cols] * jnp.exp2((old - new) * LOG2E) + part
        top[h, :, cols] = new

    def place_queries(src, lo):
        for h in range(HEADS):
            scaled = src[pl.ds(h * HD, HD), :] * jnp.bfloat16(1.0 / math.sqrt(HD))
            qs[h, pl.ds(0, HD), pl.ds(lo, TOK)] = scaled
            qs[h, pl.ds(HD, HD), pl.ds(lo, TOK)] = jnp.zeros((HD, TOK), jnp.bfloat16)

    place_queries(qb, 0)
    loads[2].wait()

    def own_fresh(h, carry):
        first(h, fresh[h], 0)
        return carry

    lax.fori_loop(0, HEADS, own_fresh, 0)

    loads[3].wait()
    for h in range(HEADS):
        for k in range(8):
            pair = [wb[:, pl.ds((2 * k + e) * HEADS * HD + h * HD, HD)] for e in range(2)]
            wp[h, :, pl.ds(k * 128, 128)] = jnp.concatenate(pair, axis=1)

    q_move.wait_recv()
    place_queries(qx, TOK)

    def own_stale(h, carry):
        first(h, kv[h, 0], TOK)
        return carry

    lax.fori_loop(0, HEADS, own_stale, 0)

    def ring_step(t, carry):
        s, h, part = 1 + t // (2 * HEADS), (t // 2) % HEADS, t % 2
        hop_right(h, part, s - 1).wait_recv()

        @pl.when(s < RIGHT_HOPS)
        def _():
            hop_right(h, part, s).start()

        hop_left(h, part, s - 1).wait_recv()
        hop_left(h, part, s).start()
        rows = pl.ds(part * HALF, HALF)
        update(h, jnp.concatenate([kv[h, s, rows], kv[h, RING - s, rows]], axis=0), 0, 2 * TOK)
        return carry

    lax.fori_loop(0, RIGHT_HOPS * HEADS * 2, ring_step, 0)

    def o_moves(h):
        return (remote(opart.at[h], oin.at[h], y_send.at[1 + h], y_recv.at[1 + h], across),
                remote(ostat.at[h], ostat_in.at[h], y_send.at[4 + h], y_recv.at[4 + h], across))

    def last_step(h, carry):
        for part in range(2):
            hop_left(h, part, LEFT_HOPS - 1).wait_recv()
        block = kv[h, RING - LEFT_HOPS]
        update(h, block, TOK, TOK)
        cols = pl.ds(TOK, TOK)
        total = acc[h, pl.ds(0, 8), cols][0:1]
        opart[h] = (acc[h, pl.ds(16, HD), cols] / total).astype(jnp.bfloat16)
        ostat[h, pl.ds(0, 1)] = top[h, :, cols]
        ostat[h, pl.ds(1, 1)] = total
        for move in o_moves(h):
            move.start()
        update(h, block, 0, TOK)
        return carry

    ostat[...] = jnp.zeros_like(ostat)
    lax.fori_loop(0, HEADS, last_step, 0)

    def sent(t, carry):
        s, h = t // HEADS, t % HEADS
        for part in range(2):
            hop_left(h, part, s).wait_send()

            @pl.when(s < RIGHT_HOPS)
            def _():
                hop_right(h, part, s).wait_send()

        return carry

    lax.fori_loop(0, LEFT_HOPS * HEADS, sent, 0)
    q_move.wait_send()

    def g_move(h, j):
        return remote(att.at[h, head], att.at[h, head], g_send.at[h, j], g_recv.at[h, j], plane(j))

    def c_move(h, j):
        slot = plane_back(j)
        return remote(att.at[h, slot], att.at[h, slot], c_send.at[h, j], c_recv.at[h, j], sibling)

    def combine(h, carry):
        for move in o_moves(h):
            move.wait_recv()
        cols = pl.ds(0, TOK)
        top_a, top_b = top[h, :, cols], ostat_in[h, pl.ds(0, 1)]
        new = jnp.maximum(top_a, top_b)
        scale_a = jnp.exp2((top_a - new) * LOG2E)
        total_a = acc[h, pl.ds(0, 8), cols][0:1] * scale_a
        total_b = ostat_in[h, pl.ds(1, 1)] * jnp.exp2((top_b - new) * LOG2E)
        inverse = 1.0 / (total_a + total_b)
        mixed = (acc[h, pl.ds(16, HD), cols] * (scale_a * inverse)
                 + oin[h].astype(jnp.float32) * (total_b * inverse))
        att[h, head] = mixed.astype(jnp.bfloat16)
        for j in (6, 5, 7, 4, 2, 1, 3):
            g_move(h, j).start()
        c_move(h, 0).start()
        return carry

    lax.fori_loop(0, HEADS, combine, 0)

    def drain(h):
        for move in o_moves(h):
            move.wait_send()
        for j in range(1, 8):
            g_move(h, j).wait_send()
        for j in range(8):
            c_move(h, j).wait_send()

    def project(h, carry):
        @pl.when(h > 0)
        def _():
            drain(h - 1)

        for j in (1, 3, 2, 4, 5, 7, 6):
            g_move(h, j).wait_recv()
            c_move(h, j).start()
        for j in range(8):
            c_move(h, j).wait_recv()
        part = jnp.dot(wp[h], att[h].reshape(16 * HD, TOK), preferred_element_type=jnp.float32)
        out[...] = out[...] + part
        return carry

    out[...] = jnp.zeros_like(out)
    lax.fori_loop(0, HEADS, project, 0)
    drain(HEADS - 1)


def on_device(queries, fresh_kv, stale_kv, residual, gate, w_out):
    bf16, f32 = jnp.bfloat16, jnp.float32
    in_hbm = pl.BlockSpec(memory_space=pltpu.HBM)
    dma = pltpu.SemaphoreType.DMA
    operands = (queries, fresh_kv.transpose(1, 0, 2), stale_kv.transpose(1, 0, 2), w_out)
    projected = pl.pallas_call(
        fused,
        out_shape=jax.ShapeDtypeStruct((HEADS * HD, TOK), f32),
        in_specs=[in_hbm] * 4,
        out_specs=pl.BlockSpec(memory_space=pltpu.VMEM),
        scratch_shapes=[
            pltpu.VMEM((HEADS, RING, TOK, 2 * HD), bf16),
            pltpu.VMEM((HEADS, TOK, 2 * HD), bf16),
            pltpu.VMEM((HEADS * HD, TOK), bf16),
            pltpu.VMEM((HEADS * HD, TOK), bf16),
            pltpu.VMEM((HEADS * HD, 16 * HEADS * HD), bf16),
            pltpu.VMEM((HEADS, HEADS * HD, 16 * HD), bf16),
            pltpu.VMEM((HEADS, 2 * HD, 2 * TOK), bf16),
            pltpu.VMEM((HEADS, ROWS, 2 * TOK), f32),
            pltpu.VMEM((HEADS, 1, 2 * TOK), f32),
            pltpu.VMEM((HEADS, HD, TOK), bf16),
            pltpu.VMEM((HEADS, 8, TOK), f32),
            pltpu.VMEM((HEADS, HD, TOK), bf16),
            pltpu.VMEM((HEADS, 8, TOK), f32),
            pltpu.VMEM((HEADS, 16, HD, TOK), bf16),
            dma((4,)),
            dma((2, HEADS, 2, LEFT_HOPS)),
            dma((2, HEADS, 2, LEFT_HOPS)),
            dma((7,)),
            dma((7,)),
            dma((HEADS, 8)),
            dma((HEADS, 8)),
            dma((HEADS, 8)),
            dma((HEADS, 8)),
        ],
        compiler_params=pltpu.CompilerParams(
            collective_id=0, has_side_effects=True, vmem_limit_bytes=40 * 1024 * 1024),
        cost_estimate=pl.CostEstimate(
            flops=2_000_000_000, bytes_accessed=4_000_000, transcendentals=6_500_000),
    )(*[pltpu.with_memory_space_constraint(operand, pltpu.HBM) for operand in operands])
    result = residual.astype(f32) + gate[:, None] * projected
    return result.astype(bf16)


def solution(mesh):
    placed = (
        P("head", "patch"),
        P("patch", "head", None),
        P("patch", "head", None),
        P("head", "patch"),
        P("head"),
        P("head", None),
    )
    return jax.shard_map(
        on_device, mesh=mesh, in_specs=placed, out_specs=P("head", "patch"), check_vma=False
    )
```

```python
import functools
import math

import jax
import jax.numpy as jnp
from jax import lax
from jax.experimental import pallas as pl
from jax.experimental.pallas import tpu as pltpu
from jax.sharding import PartitionSpec as P

MESH = pl.DeviceIdType.MESH
HEADS = 3
HD = 64
TOK = 256
RING = 16
LOG2E = 1.4426950408889634
HALF = TOK // 2
RIGHT_HOPS, LEFT_HOPS = 7, 8
ROWS = HD + 16


def fused(q_in, fresh_in, stale_in, w_in, out, kv, fresh, qb, qx, wb, wp, qs, acc, top,
          opart, ostat, oin, ostat_in, att, load_sem, z_send, z_recv, y_send, y_recv,
          g_send, g_recv, c_send, c_recv):
    patch = lax.axis_index("patch")
    head = lax.axis_index("head")
    y_lo, z = patch // RING, patch % RING
    y_hi, x, core = head // 8, (head // 2) % 4, head % 2
    right = (y_lo * RING + (z + 1) % RING, head)
    left = (y_lo * RING + (z + RING - 1) % RING, head)
    across = ((1 - y_lo) * RING + z, head)
    sibling = (patch, head + 1 - 2 * core)

    def plane(j):
        return (patch, ((y_hi + j // 4) % 2) * 8 + ((x + j % 4) % 4) * 2 + core)

    def plane_back(j):
        return ((y_hi + j // 4) % 2) * 8 + ((x + 4 - j % 4) % 4) * 2 + core

    loads = [
        pltpu.make_async_copy(stale_in, kv.at[:, 0], load_sem.at[0]),
        pltpu.make_async_copy(q_in, qb, load_sem.at[1]),
        pltpu.make_async_copy(fresh_in, fresh, load_sem.at[2]),
        pltpu.make_async_copy(w_in, wb, load_sem.at[3]),
    ]
    for load in loads:
        load.start()

    barrier = pltpu.get_barrier_semaphore()
    partners = [right, left, across, sibling] + [plane(j) for j in range(1, 8)]
    for partner in partners:
        pl.semaphore_signal(barrier, inc=1, device_id=partner, device_id_type=MESH)
    pl.semaphore_wait(barrier, len(partners))

    def remote(src, dst, send, recv, device):
        return pltpu.make_async_remote_copy(
            src_ref=src, dst_ref=dst, send_sem=send, recv_sem=recv,
            device_id=device, device_id_type=MESH)

    def hop_right(h, part, s):
        rows = pl.ds(part * HALF, HALF)
        return remote(kv.at[h, s, rows], kv.at[h, s + 1, rows], z_send.at[0, h, part, s],
                      z_recv.at[0, h, part, s], right)

    def hop_left(h, part, s):
        rows = pl.ds(part * HALF, HALF)
        return remote(kv.at[h, (RING - s) % RING, rows], kv.at[h, RING - 1 - s, rows],
                      z_send.at[1, h, part, s], z_recv.at[1, h, part, s], left)

    loads[0].wait()
    for h in range(HEADS):
        for part in range(2):
            hop_right(h, part, 0).start()
            hop_left(h, part, 0).start()
    loads[1].wait()
    q_move = remote(qb, qx, y_send.at[0], y_recv.at[0], across)
    q_move.start()

    lane = lax.broadcasted_iota(jnp.int32, (1, 2 * HD), 1)

    def with_ones(block):
        swapped = jnp.where(lane < HD, jnp.ones_like(block), block)
        return swapped.T[HD - 16:]

    def first(h, block, lo):
        cols = pl.ds(lo, TOK)
        scores = jnp.dot(block, qs[h, :, cols], preferred_element_type=jnp.float32)
        high_score = jnp.max(scores, axis=0, keepdims=True)
        weights = jnp.exp2((scores - high_score) * LOG2E).astype(jnp.bfloat16)
        acc[h, :, cols] = jnp.dot(with_ones(block), weights, preferred_element_type=jnp.float32)
        top[h, :, cols] = high_score

    def update(h, block, lo, width):
        cols = pl.ds(lo, width)
        scores = jnp.dot(block, qs[h, :, cols], preferred_element_type=jnp.float32)
        old = top[h, :, cols]
        new = jnp.maximum(old, jnp.max(scores, axis=0, keepdims=True))
        weights = jnp.exp2((scores - new) * LOG2E).astype(jnp.bfloat16)
        part = jnp.dot(with_ones(block), weights, preferred_element_type=jnp.float32)
        acc[h, :, cols] = acc[h, :, cols] * jnp.exp2((old - new) * LOG2E) + part
        top[h, :, cols] = new

    def place_queries(src, lo):
        for h in range(HEADS):
            scaled = src[pl.ds(h * HD, HD), :] * jnp.bfloat16(1.0 / math.sqrt(HD))
            qs[h, pl.ds(0, HD), pl.ds(lo, TOK)] = scaled
            qs[h, pl.ds(HD, HD), pl.ds(lo, TOK)] = jnp.zeros((HD, TOK), jnp.bfloat16)

    place_queries(qb, 0)
    loads[2].wait()

    def own_fresh(h, carry):
        first(h, fresh[h], 0)
        return carry

    lax.fori_loop(0, HEADS, own_fresh, 0)

    loads[3].wait()
    for h in range(HEADS):
        for k in range(8):
            pair = [wb[:, pl.ds((2 * k + e) * HEADS * HD + h * HD, HD)] for e in range(2)]
            wp[h, :, pl.ds(k * 128, 128)] = jnp.concatenate(pair, axis=1)

    lead = (1 - (z + 9) // RING) * (2 * HEADS - z)

    def piece(u):
        return 1 + u // (2 * HEADS), (u // 2) % HEADS, u % 2

    def land_right(t):
        u = t - lead
        s, h, part = piece(u)

        @pl.when((u >= 0) & (u < RIGHT_HOPS * 2 * HEADS))
        def _():
            hop_right(h, part, s - 1).wait_recv()

            @pl.when(s < RIGHT_HOPS)
            def _():
                hop_right(h, part, s).start()

    def land_left(t):
        s, h, part = piece(t)
        hop_left(h, part, s - 1).wait_recv()

        @pl.when(s < LEFT_HOPS)
        def _():
            hop_left(h, part, s).start()

    def attend_right(t):
        u = t - lead
        s, h, part = piece(u)

        @pl.when((u >= 0) & (u < RIGHT_HOPS * 2 * HEADS) & (part == 1))
        def _():
            update(h, kv[h, s], 0, 2 * TOK)

    def attend_left(t):
        s, h, part = piece(t)

        @pl.when(part == 1)
        def _():
            update(h, kv[h, RING - s], 0, 2 * TOK)

    def pass_on(t, carry):
        land_right(t)
        land_left(t)
        return carry

    lax.fori_loop(0, HEADS, pass_on, 0)
    q_move.wait_recv()
    place_queries(qx, TOK)

    def own_stale(h, carry):
        pass_on(HEADS + h, 0)
        first(h, kv[h, 0], TOK)
        return carry

    lax.fori_loop(0, HEADS, own_stale, 0)

    def ring_step(t, carry):
        land_right(t)
        land_left(t)
        attend_right(t)
        attend_left(t)
        late = t // 4 - 1
        h, side = late // 2, late % 2

        @pl.when((t % 4 == 2) & (late < 2 * HEADS) & ((side == 0) | (2 * h + 1 + lead < 2 * HEADS)))
        def _():
            update(h, kv[h, 15 - 14 * side], 0, 2 * TOK)

        return carry

    lax.fori_loop(2 * HEADS, (LEFT_HOPS - 1) * 2 * HEADS, ring_step, 0)

    def o_moves(h):
        return (remote(opart.at[h], oin.at[h], y_send.at[1 + h], y_recv.at[1 + h], across),
                remote(ostat.at[h], ostat_in.at[h], y_send.at[4 + h], y_recv.at[4 + h], across))

    def last_step(h, carry):
        def arrive(part, inner):
            t = (LEFT_HOPS - 1) * 2 * HEADS + 2 * h + part
            pass_on(t, 0)
            attend_right(t)
            return inner

        lax.fori_loop(0, 2, arrive, 0)
        block = kv[h, RING - LEFT_HOPS]
        update(h, block, TOK, TOK)
        cols = pl.ds(TOK, TOK)
        total = acc[h, pl.ds(0, 8), cols][0:1]
        opart[h] = (acc[h, pl.ds(16, HD), cols] / total).astype(jnp.bfloat16)
        ostat[h, pl.ds(0, 1)] = top[h, :, cols]
        ostat[h, pl.ds(1, 1)] = total
        for move in o_moves(h):
            move.start()
        update(h, block, 0, TOK)
        return carry

    ostat[...] = jnp.zeros_like(ostat)
    lax.fori_loop(0, HEADS, last_step, 0)

    def sent(t, carry):
        s, h = t // HEADS, t % HEADS
        for part in range(2):
            hop_left(h, part, s).wait_send()

            @pl.when(s < RIGHT_HOPS)
            def _():
                hop_right(h, part, s).wait_send()

        return carry

    lax.fori_loop(0, LEFT_HOPS * HEADS, sent, 0)
    q_move.wait_send()

    def g_move(h, j):
        return remote(att.at[h, head], att.at[h, head], g_send.at[h, j], g_recv.at[h, j], plane(j))

    def c_move(h, j):
        slot = plane_back(j)
        return remote(att.at[h, slot], att.at[h, slot], c_send.at[h, j], c_recv.at[h, j], sibling)

    def combine(h, carry):
        for move in o_moves(h):
            move.wait_recv()
        cols = pl.ds(0, TOK)
        top_a, top_b = top[h, :, cols], ostat_in[h, pl.ds(0, 1)]
        new = jnp.maximum(top_a, top_b)
        scale_a = jnp.exp2((top_a - new) * LOG2E)
        total_a = acc[h, pl.ds(0, 8), cols][0:1] * scale_a
        total_b = ostat_in[h, pl.ds(1, 1)] * jnp.exp2((top_b - new) * LOG2E)
        inverse = 1.0 / (total_a + total_b)
        mixed = (acc[h, pl.ds(16, HD), cols] * (scale_a * inverse)
                 + oin[h].astype(jnp.float32) * (total_b * inverse))
        att[h, head] = mixed.astype(jnp.bfloat16)
        for j in (1, 3, 4, 2, 5, 7, 6):
            g_move(h, j).start()
        c_move(h, 0).start()
        return carry

    lax.fori_loop(0, HEADS, combine, 0)

    def drain(h):
        for move in o_moves(h):
            move.wait_send()
        for j in range(1, 8):
            g_move(h, j).wait_send()
        for j in range(8):
            c_move(h, j).wait_send()

    def project(h, carry):
        @pl.when(h > 0)
        def _():
            drain(h - 1)

        for j in (1, 3, 4, 2, 5, 7, 6):
            g_move(h, j).wait_recv()
            c_move(h, j).start()
        for j in range(8):
            c_move(h, j).wait_recv()
        part = jnp.dot(wp[h], att[h].reshape(16 * HD, TOK), preferred_element_type=jnp.float32)
        out[...] = out[...] + part
        return carry

    out[...] = jnp.zeros_like(out)
    lax.fori_loop(0, HEADS, project, 0)
    drain(HEADS - 1)


def on_device(queries, fresh_kv, stale_kv, residual, gate, w_out):
    bf16, f32 = jnp.bfloat16, jnp.float32
    in_hbm = pl.BlockSpec(memory_space=pltpu.HBM)
    dma = pltpu.SemaphoreType.DMA
    operands = (queries, fresh_kv.transpose(1, 0, 2), stale_kv.transpose(1, 0, 2), w_out)
    projected = pl.pallas_call(
        fused,
        out_shape=jax.ShapeDtypeStruct((HEADS * HD, TOK), f32),
        in_specs=[in_hbm] * 4,
        out_specs=pl.BlockSpec(memory_space=pltpu.VMEM),
        scratch_shapes=[
            pltpu.VMEM((HEADS, RING, TOK, 2 * HD), bf16),
            pltpu.VMEM((HEADS, TOK, 2 * HD), bf16),
            pltpu.VMEM((HEADS * HD, TOK), bf16),
            pltpu.VMEM((HEADS * HD, TOK), bf16),
            pltpu.VMEM((HEADS * HD, 16 * HEADS * HD), bf16),
            pltpu.VMEM((HEADS, HEADS * HD, 16 * HD), bf16),
            pltpu.VMEM((HEADS, 2 * HD, 2 * TOK), bf16),
            pltpu.VMEM((HEADS, ROWS, 2 * TOK), f32),
            pltpu.VMEM((HEADS, 1, 2 * TOK), f32),
            pltpu.VMEM((HEADS, HD, TOK), bf16),
            pltpu.VMEM((HEADS, 8, TOK), f32),
            pltpu.VMEM((HEADS, HD, TOK), bf16),
            pltpu.VMEM((HEADS, 8, TOK), f32),
            pltpu.VMEM((HEADS, 16, HD, TOK), bf16),
            dma((4,)),
            dma((2, HEADS, 2, LEFT_HOPS)),
            dma((2, HEADS, 2, LEFT_HOPS)),
            dma((7,)),
            dma((7,)),
            dma((HEADS, 8)),
            dma((HEADS, 8)),
            dma((HEADS, 8)),
            dma((HEADS, 8)),
        ],
        compiler_params=pltpu.CompilerParams(
            collective_id=0, has_side_effects=True, vmem_limit_bytes=40 * 1024 * 1024),
        cost_estimate=pl.CostEstimate(
            flops=2_000_000_000, bytes_accessed=4_000_000, transcendentals=6_500_000),
    )(*[pltpu.with_memory_space_constraint(operand, pltpu.HBM) for operand in operands])
    result = residual.astype(f32) + gate[:, None] * projected
    return result.astype(bf16)


def solution(mesh):
    placed = (
        P("head", "patch"),
        P("patch", "head", None),
        P("patch", "head", None),
        P("head", "patch"),
        P("head"),
        P("head", None),
    )
    return jax.shard_map(
        on_device, mesh=mesh, in_specs=placed, out_specs=P("head", "patch"), check_vma=False
    )
```

```python
import functools
import math

import jax
import jax.numpy as jnp
from jax import lax
from jax.experimental import pallas as pl
from jax.experimental.pallas import tpu as pltpu
from jax.sharding import PartitionSpec as P

MESH = pl.DeviceIdType.MESH
HEADS = 3
HD = 64
TOK = 256
RING = 16
LOG2E = 1.4426950408889634
HALF = TOK // 2
RIGHT_HOPS, LEFT_HOPS = 7, 8
ROWS = HD + 16


def fused(q_in, fresh_in, stale_in, w_in, out, kv, fresh, qb, qx, wb, wp, qs, acc, top,
          opart, ostat, oin, ostat_in, att, load_sem, z_send, z_recv, y_send, y_recv,
          g_send, g_recv, c_send, c_recv):
    patch = lax.axis_index("patch")
    head = lax.axis_index("head")
    y_lo, z = patch // RING, patch % RING
    y_hi, x, core = head // 8, (head // 2) % 4, head % 2
    right = (y_lo * RING + (z + 1) % RING, head)
    left = (y_lo * RING + (z + RING - 1) % RING, head)
    across = ((1 - y_lo) * RING + z, head)
    sibling = (patch, head + 1 - 2 * core)

    def plane(j):
        return (patch, ((y_hi + j // 4) % 2) * 8 + ((x + j % 4) % 4) * 2 + core)

    def plane_back(j):
        return ((y_hi + j // 4) % 2) * 8 + ((x + 4 - j % 4) % 4) * 2 + core

    loads = [
        pltpu.make_async_copy(stale_in, kv.at[:, 0], load_sem.at[0]),
        pltpu.make_async_copy(q_in, qb, load_sem.at[1]),
        pltpu.make_async_copy(fresh_in, fresh, load_sem.at[2]),
        pltpu.make_async_copy(w_in, wb, load_sem.at[3]),
    ]
    for load in loads:
        load.start()

    barrier = pltpu.get_barrier_semaphore()
    partners = [right, left, across, sibling] + [plane(j) for j in range(1, 8)]
    for partner in partners:
        pl.semaphore_signal(barrier, inc=1, device_id=partner, device_id_type=MESH)
    pl.semaphore_wait(barrier, len(partners))

    def remote(src, dst, send, recv, device):
        return pltpu.make_async_remote_copy(
            src_ref=src, dst_ref=dst, send_sem=send, recv_sem=recv,
            device_id=device, device_id_type=MESH)

    def hop_right(h, part, s):
        rows = pl.ds(part * HALF, HALF)
        return remote(kv.at[h, s, rows], kv.at[h, s + 1, rows], z_send.at[0, h, part, s],
                      z_recv.at[0, h, part, s], right)

    def hop_left(h, part, s):
        rows = pl.ds(part * HALF, HALF)
        return remote(kv.at[h, (RING - s) % RING, rows], kv.at[h, RING - 1 - s, rows],
                      z_send.at[1, h, part, s], z_recv.at[1, h, part, s], left)

    loads[0].wait()
    for h in range(HEADS):
        for part in range(2):
            hop_right(h, part, 0).start()
            hop_left(h, part, 0).start()
    loads[1].wait()
    q_move = remote(qb, qx, y_send.at[0], y_recv.at[0], across)
    q_move.start()

    lane = lax.broadcasted_iota(jnp.int32, (1, 2 * HD), 1)

    def with_ones(block):
        swapped = jnp.where(lane < HD, jnp.ones_like(block), block)
        return swapped.T[HD - 16:]

    def first(h, block, lo):
        cols = pl.ds(lo, TOK)
        scores = jnp.dot(block, qs[h, :, cols], preferred_element_type=jnp.float32)
        high_score = jnp.max(scores, axis=0, keepdims=True)
        weights = jnp.exp2((scores - high_score) * LOG2E).astype(jnp.bfloat16)
        acc[h, :, cols] = jnp.dot(with_ones(block), weights, preferred_element_type=jnp.float32)
        top[h, :, cols] = high_score

    def update(h, block, lo, width):
        cols = pl.ds(lo, width)
        scores = jnp.dot(block, qs[h, :, cols], preferred_element_type=jnp.float32)
        old = top[h, :, cols]
        new = jnp.maximum(old, jnp.max(scores, axis=0, keepdims=True))
        weights = jnp.exp2((scores - new) * LOG2E).astype(jnp.bfloat16)
        part = jnp.dot(with_ones(block), weights, preferred_element_type=jnp.float32)
        acc[h, :, cols] = acc[h, :, cols] * jnp.exp2((old - new) * LOG2E) + part
        top[h, :, cols] = new

    def place_queries(src, lo):
        for h in range(HEADS):
            scaled = src[pl.ds(h * HD, HD), :] * jnp.bfloat16(1.0 / math.sqrt(HD))
            qs[h, pl.ds(0, HD), pl.ds(lo, TOK)] = scaled
            qs[h, pl.ds(HD, HD), pl.ds(lo, TOK)] = jnp.zeros((HD, TOK), jnp.bfloat16)

    place_queries(qb, 0)
    loads[2].wait()

    def own_fresh(h, carry):
        first(h, fresh[h], 0)
        return carry

    lax.fori_loop(0, HEADS, own_fresh, 0)

    loads[3].wait()
    for h in range(HEADS):
        for k in range(8):
            pair = [wb[:, pl.ds((2 * k + e) * HEADS * HD + h * HD, HD)] for e in range(2)]
            wp[h, :, pl.ds(k * 128, 128)] = jnp.concatenate(pair, axis=1)

    lead = (1 - (z + 9) // RING) * (2 * HEADS - z)

    def piece(u):
        return 1 + u // (2 * HEADS), (u // 2) % HEADS, u % 2

    def land_right(t):
        u = t - lead
        s, h, part = piece(u)

        @pl.when((u >= 0) & (u < RIGHT_HOPS * 2 * HEADS))
        def _():
            hop_right(h, part, s - 1).wait_recv()

            @pl.when(s < RIGHT_HOPS)
            def _():
                hop_right(h, part, s).start()

            @pl.when(s >= 2)
            def _():
                hop_right(h, part, s - 2).wait_send()

    def land_left(t):
        s, h, part = piece(t)
        hop_left(h, part, s - 1).wait_recv()

        @pl.when(s < LEFT_HOPS)
        def _():
            hop_left(h, part, s).start()

        @pl.when(s >= 2)
        def _():
            hop_left(h, part, s - 2).wait_send()

    def attend_right(t):
        u = t - lead
        s, h, part = piece(u)

        @pl.when((u >= 0) & (s < RIGHT_HOPS) & (part == 1))
        def _():
            update(h, kv[h, s], 0, 2 * TOK)

    def attend_left(t):
        s, h, part = piece(t)

        @pl.when(part == 1)
        def _():
            update(h, kv[h, RING - s], 0, 2 * TOK)

    def pass_on(t, carry):
        land_right(t)
        land_left(t)
        return carry

    lax.fori_loop(0, HEADS, pass_on, 0)
    q_move.wait_recv()
    place_queries(qx, TOK)

    def own_stale(h, carry):
        pass_on(HEADS + h, 0)
        first(h, kv[h, 0], TOK)
        return carry

    lax.fori_loop(0, HEADS, own_stale, 0)

    def ring_step(t, carry):
        land_right(t)
        land_left(t)
        attend_right(t)
        attend_left(t)
        late = t // 4 - 1
        h, side = late // 2, late % 2

        @pl.when((t % 4 == 2) & (late < 2 * HEADS) & ((side == 0) | (2 * h + 1 + lead < 2 * HEADS)))
        def _():
            update(h, kv[h, 15 - 14 * side], 0, 2 * TOK)

        return carry

    lax.fori_loop(2 * HEADS, (LEFT_HOPS - 1) * 2 * HEADS, ring_step, 0)

    def o_moves(h):
        return (remote(opart.at[h], oin.at[h], y_send.at[1 + h], y_recv.at[1 + h], across),
                remote(ostat.at[h], ostat_in.at[h], y_send.at[4 + h], y_recv.at[4 + h], across))

    def last_step(h, carry):
        def last_rows(part):
            rows = pl.ds(part * HALF, HALF)
            return jnp.concatenate(
                [kv[h, RIGHT_HOPS, rows], kv[h, RING - LEFT_HOPS, rows]], axis=0)

        t = (LEFT_HOPS - 1) * 2 * HEADS + 2 * h
        pass_on(t, 0)
        update(h, last_rows(0), 0, 2 * TOK)
        pass_on(t + 1, 0)
        block = last_rows(1)
        update(h, block, TOK, TOK)
        cols = pl.ds(TOK, TOK)
        total = acc[h, pl.ds(0, 8), cols][0:1]
        opart[h] = (acc[h, pl.ds(16, HD), cols] / total).astype(jnp.bfloat16)
        ostat[h, pl.ds(0, 1)] = top[h, :, cols]
        ostat[h, pl.ds(1, 1)] = total
        for move in o_moves(h):
            move.start()
        update(h, block, 0, TOK)
        return carry

    lax.fori_loop(0, HEADS, last_step, 0)

    def g_move(h, j):
        return remote(att.at[h, head], att.at[h, head], g_send.at[h, j], g_recv.at[h, j], plane(j))

    def c_move(h, j):
        slot = plane_back(j)
        return remote(att.at[h, slot], att.at[h, slot], c_send.at[h, j], c_recv.at[h, j], sibling)

    def combine(h, carry):
        for move in o_moves(h):
            move.wait_recv()
        cols = pl.ds(0, TOK)
        top_a, top_b = top[h, :, cols], ostat_in[h, pl.ds(0, 1)]
        new = jnp.maximum(top_a, top_b)
        scale_a = jnp.exp2((top_a - new) * LOG2E)
        total_a = acc[h, pl.ds(0, 8), cols][0:1] * scale_a
        total_b = ostat_in[h, pl.ds(1, 1)] * jnp.exp2((top_b - new) * LOG2E)
        inverse = 1.0 / (total_a + total_b)
        mixed = (acc[h, pl.ds(16, HD), cols] * (scale_a * inverse)
                 + oin[h].astype(jnp.float32) * (total_b * inverse))
        att[h, head] = mixed.astype(jnp.bfloat16)
        for j in (1, 3, 4, 2, 5, 7, 6):
            g_move(h, j).start()
        c_move(h, 0).start()
        return carry

    lax.fori_loop(0, HEADS, combine, 0)

    def sent(t, carry):
        hop_right(t // 2, t % 2, RIGHT_HOPS - 1).wait_send()
        hop_left(t // 2, t % 2, LEFT_HOPS - 1).wait_send()
        return carry

    lax.fori_loop(0, 2 * HEADS, sent, 0)
    q_move.wait_send()

    def drain(h):
        for j in range(8):
            c_move(h, j).wait_send()

    def project(h, carry):
        @pl.when(h > 0)
        def _():
            drain(h - 1)

        for j in (1, 3, 4, 2, 5, 7, 6):
            g_move(h, j).wait_recv()
            c_move(h, j).start()
        for j in range(1, 8):
            g_move(h, j).wait_send()
        for move in o_moves(h):
            move.wait_send()
        for j in range(8):
            c_move(h, j).wait_recv()
        part = jnp.dot(wp[h], att[h].reshape(16 * HD, TOK), preferred_element_type=jnp.float32)
        out[...] = out[...] + part
        return carry

    out[...] = jnp.zeros_like(out)
    lax.fori_loop(0, HEADS, project, 0)
    drain(HEADS - 1)


def on_device(queries, fresh_kv, stale_kv, residual, gate, w_out):
    bf16, f32 = jnp.bfloat16, jnp.float32
    in_hbm = pl.BlockSpec(memory_space=pltpu.HBM)
    dma = pltpu.SemaphoreType.DMA
    operands = (queries, fresh_kv.transpose(1, 0, 2), stale_kv.transpose(1, 0, 2), w_out)
    projected = pl.pallas_call(
        fused,
        out_shape=jax.ShapeDtypeStruct((HEADS * HD, TOK), f32),
        in_specs=[in_hbm] * 4,
        out_specs=pl.BlockSpec(memory_space=pltpu.VMEM),
        scratch_shapes=[
            pltpu.VMEM((HEADS, RING, TOK, 2 * HD), bf16),
            pltpu.VMEM((HEADS, TOK, 2 * HD), bf16),
            pltpu.VMEM((HEADS * HD, TOK), bf16),
            pltpu.VMEM((HEADS * HD, TOK), bf16),
            pltpu.VMEM((HEADS * HD, 16 * HEADS * HD), bf16),
            pltpu.VMEM((HEADS, HEADS * HD, 16 * HD), bf16),
            pltpu.VMEM((HEADS, 2 * HD, 2 * TOK), bf16),
            pltpu.VMEM((HEADS, ROWS, 2 * TOK), f32),
            pltpu.VMEM((HEADS, 1, 2 * TOK), f32),
            pltpu.VMEM((HEADS, HD, TOK), bf16),
            pltpu.VMEM((HEADS, 2, TOK), f32),
            pltpu.VMEM((HEADS, HD, TOK), bf16),
            pltpu.VMEM((HEADS, 2, TOK), f32),
            pltpu.VMEM((HEADS, 16, HD, TOK), bf16),
            dma((4,)),
            dma((2, HEADS, 2, LEFT_HOPS)),
            dma((2, HEADS, 2, LEFT_HOPS)),
            dma((7,)),
            dma((7,)),
            dma((HEADS, 8)),
            dma((HEADS, 8)),
            dma((HEADS, 8)),
            dma((HEADS, 8)),
        ],
        compiler_params=pltpu.CompilerParams(
            collective_id=0, has_side_effects=True, vmem_limit_bytes=40 * 1024 * 1024),
        cost_estimate=pl.CostEstimate(
            flops=2_000_000_000, bytes_accessed=4_000_000, transcendentals=6_500_000),
    )(*[pltpu.with_memory_space_constraint(operand, pltpu.HBM) for operand in operands])
    result = residual.astype(f32) + gate[:, None] * projected
    return result.astype(bf16)


def solution(mesh):
    placed = (
        P("head", "patch"),
        P("patch", "head", None),
        P("patch", "head", None),
        P("head", "patch"),
        P("head"),
        P("head", None),
    )
    return jax.shard_map(
        on_device, mesh=mesh, in_specs=placed, out_specs=P("head", "patch"), check_vma=False
    )
```

```python
import functools
import math

import jax
import jax.numpy as jnp
from jax import lax
from jax.experimental import pallas as pl
from jax.experimental.pallas import tpu as pltpu
from jax.sharding import PartitionSpec as P

MESH = pl.DeviceIdType.MESH
HEADS = 3
HD = 64
TOK = 256
RING = 16
LOG2E = 1.4426950408889634
HALF = TOK // 2
RIGHT_HOPS, LEFT_HOPS = 7, 8
ROWS = HD + 16


def fused(q_in, fresh_in, stale_in, w_in, out, kv, fresh, qb, qx, wb, wp, qs, acc, top,
          opart, ostat, oin, ostat_in, att, load_sem, z_send, z_recv, y_send, y_recv,
          g_send, g_recv, c_send, c_recv):
    patch = lax.axis_index("patch")
    head = lax.axis_index("head")
    y_lo, z = patch // RING, patch % RING
    y_hi, x, core = head // 8, (head // 2) % 4, head % 2
    right = (y_lo * RING + (z + 1) % RING, head)
    left = (y_lo * RING + (z + RING - 1) % RING, head)
    across = ((1 - y_lo) * RING + z, head)
    sibling = (patch, head + 1 - 2 * core)

    def plane(j):
        return (patch, ((y_hi + j // 4) % 2) * 8 + ((x + j % 4) % 4) * 2 + core)

    def plane_back(j):
        return ((y_hi + j // 4) % 2) * 8 + ((x + 4 - j % 4) % 4) * 2 + core

    loads = [
        pltpu.make_async_copy(stale_in, kv.at[:, 0], load_sem.at[0]),
        pltpu.make_async_copy(q_in, qb, load_sem.at[1]),
        pltpu.make_async_copy(fresh_in, fresh, load_sem.at[2]),
        pltpu.make_async_copy(w_in, wb, load_sem.at[3]),
    ]
    for load in loads:
        load.start()

    barrier = pltpu.get_barrier_semaphore()
    partners = [right, left, across, sibling] + [plane(j) for j in range(1, 8)]
    for partner in partners:
        pl.semaphore_signal(barrier, inc=1, device_id=partner, device_id_type=MESH)
    pl.semaphore_wait(barrier, len(partners))

    def remote(src, dst, send, recv, device):
        return pltpu.make_async_remote_copy(
            src_ref=src, dst_ref=dst, send_sem=send, recv_sem=recv,
            device_id=device, device_id_type=MESH)

    def hop_right(h, part, s):
        rows = pl.ds(part * HALF, HALF)
        return remote(kv.at[h, s, rows], kv.at[h, s + 1, rows], z_send.at[0, h, part, s],
                      z_recv.at[0, h, part, s], right)

    def hop_left(h, part, s):
        rows = pl.ds(part * HALF, HALF)
        return remote(kv.at[h, (RING - s) % RING, rows], kv.at[h, RING - 1 - s, rows],
                      z_send.at[1, h, part, s], z_recv.at[1, h, part, s], left)

    loads[0].wait()
    for h in range(HEADS):
        for part in range(2):
            hop_right(h, part, 0).start()
            hop_left(h, part, 0).start()
    loads[1].wait()
    q_move = remote(qb, qx, y_send.at[0], y_recv.at[0], across)
    q_move.start()

    lane = lax.broadcasted_iota(jnp.int32, (1, 2 * HD), 1)

    def with_ones(block):
        swapped = jnp.where(lane < HD, jnp.ones_like(block), block)
        return swapped.T[HD - 16:]

    def first(h, block, lo):
        cols = pl.ds(lo, TOK)
        scores = jnp.dot(block, qs[h, :, cols], preferred_element_type=jnp.float32)
        high_score = jnp.max(scores, axis=0, keepdims=True)
        weights = jnp.exp2((scores - high_score) * LOG2E).astype(jnp.bfloat16)
        acc[h, :, cols] = jnp.dot(with_ones(block), weights, preferred_element_type=jnp.float32)
        top[h, :, cols] = high_score

    def update(h, block, lo, width):
        cols = pl.ds(lo, width)
        scores = jnp.dot(block, qs[h, :, cols], preferred_element_type=jnp.float32)
        old = top[h, :, cols]
        new = jnp.maximum(old, jnp.max(scores, axis=0, keepdims=True))
        weights = jnp.exp2((scores - new) * LOG2E).astype(jnp.bfloat16)
        part = jnp.dot(with_ones(block), weights, preferred_element_type=jnp.float32)
        acc[h, :, cols] = acc[h, :, cols] * jnp.exp2((old - new) * LOG2E) + part
        top[h, :, cols] = new

    def place_queries(src, lo):
        for h in range(HEADS):
            scaled = src[pl.ds(h * HD, HD), :] * jnp.bfloat16(1.0 / math.sqrt(HD))
            qs[h, pl.ds(0, HD), pl.ds(lo, TOK)] = scaled
            qs[h, pl.ds(HD, HD), pl.ds(lo, TOK)] = jnp.zeros((HD, TOK), jnp.bfloat16)

    place_queries(qb, 0)
    loads[2].wait()

    def own_fresh(h, carry):
        first(h, fresh[h], 0)
        return carry

    lax.fori_loop(0, HEADS, own_fresh, 0)

    loads[3].wait()
    for h in range(HEADS):
        for k in range(8):
            pair = [wb[:, pl.ds((2 * k + e) * HEADS * HD + h * HD, HD)] for e in range(2)]
            wp[h, :, pl.ds(k * 128, 128)] = jnp.concatenate(pair, axis=1)

    lead = (1 - (z + 9) // RING) * (2 * HEADS - z)

    def piece(u):
        return 1 + u // (2 * HEADS), (u // 2) % HEADS, u % 2

    def land_right(t):
        u = t - lead
        s, h, part = piece(u)

        @pl.when((u >= 0) & (u < RIGHT_HOPS * 2 * HEADS))
        def _():
            hop_right(h, part, s - 1).wait_recv()

            @pl.when(s < RIGHT_HOPS)
            def _():
                hop_right(h, part, s).start()

            @pl.when(s >= 2)
            def _():
                hop_right(h, part, s - 2).wait_send()

    def land_left(t):
        s, h, part = piece(t)
        hop_left(h, part, s - 1).wait_recv()

        @pl.when(s < LEFT_HOPS)
        def _():
            hop_left(h, part, s).start()

        @pl.when(s >= 2)
        def _():
            hop_left(h, part, s - 2).wait_send()

    def attend_right(t):
        u = t - lead
        s, h, part = piece(u)

        @pl.when((u >= 0) & (s < RIGHT_HOPS) & (part == 1))
        def _():
            update(h, kv[h, s], 0, 2 * TOK)

    def attend_left(t):
        s, h, part = piece(t)

        @pl.when(part == 1)
        def _():
            update(h, kv[h, RING - s], 0, 2 * TOK)

    def pass_on(t, carry):
        land_left(t)
        land_right(t)
        return carry

    lax.fori_loop(0, HEADS, pass_on, 0)
    q_move.wait_recv()
    place_queries(qx, TOK)

    def own_stale(h, carry):
        pass_on(HEADS + h, 0)
        first(h, kv[h, 0], TOK)
        return carry

    lax.fori_loop(0, HEADS, own_stale, 0)

    def ring_step(t, carry):
        land_left(t)
        land_right(t)
        attend_right(t)
        attend_left(t)
        late = t // 4 - 1
        h, side = late // 2, late % 2

        @pl.when((t % 4 == 2) & (late < 2 * HEADS) & ((side == 0) | (2 * h + 1 + lead < 2 * HEADS)))
        def _():
            update(h, kv[h, 15 - 14 * side], 0, 2 * TOK)

        return carry

    lax.fori_loop(2 * HEADS, (LEFT_HOPS - 1) * 2 * HEADS, ring_step, 0)

    def o_moves(h):
        return (remote(opart.at[h], oin.at[h], y_send.at[1 + h], y_recv.at[1 + h], across),
                remote(ostat.at[h], ostat_in.at[h], y_send.at[4 + h], y_recv.at[4 + h], across))

    def last_step(h, carry):
        def last_rows(part):
            rows = pl.ds(part * HALF, HALF)
            return jnp.concatenate(
                [kv[h, RIGHT_HOPS, rows], kv[h, RING - LEFT_HOPS, rows]], axis=0)

        t = (LEFT_HOPS - 1) * 2 * HEADS + 2 * h
        pass_on(t, 0)
        update(h, last_rows(0), 0, 2 * TOK)
        pass_on(t + 1, 0)
        block = last_rows(1)
        update(h, block, TOK, TOK)
        cols = pl.ds(TOK, TOK)
        total = acc[h, pl.ds(0, 8), cols][0:1]
        opart[h] = (acc[h, pl.ds(16, HD), cols] / total).astype(jnp.bfloat16)
        ostat[h, pl.ds(0, 1)] = top[h, :, cols]
        ostat[h, pl.ds(1, 1)] = total
        for move in o_moves(h):
            move.start()
        update(h, block, 0, TOK)
        return carry

    lax.fori_loop(0, HEADS, last_step, 0)

    def g_move(h, j):
        return remote(att.at[h, head], att.at[h, head], g_send.at[h, j], g_recv.at[h, j], plane(j))

    def c_move(h, j):
        slot = plane_back(j)
        return remote(att.at[h, slot], att.at[h, slot], c_send.at[h, j], c_recv.at[h, j], sibling)

    def combine(h, carry):
        for move in o_moves(h):
            move.wait_recv()
        cols = pl.ds(0, TOK)
        top_a, top_b = top[h, :, cols], ostat_in[h, pl.ds(0, 1)]
        new = jnp.maximum(top_a, top_b)
        scale_a = jnp.exp2((top_a - new) * LOG2E)
        total_a = acc[h, pl.ds(0, 8), cols][0:1] * scale_a
        total_b = ostat_in[h, pl.ds(1, 1)] * jnp.exp2((top_b - new) * LOG2E)
        inverse = 1.0 / (total_a + total_b)
        mixed = (acc[h, pl.ds(16, HD), cols] * (scale_a * inverse)
                 + oin[h].astype(jnp.float32) * (total_b * inverse))
        att[h, head] = mixed.astype(jnp.bfloat16)
        for j in (2, 1, 3, 6, 5, 7, 4):
            g_move(h, j).start()
        c_move(h, 0).start()
        return carry

    lax.fori_loop(0, HEADS, combine, 0)

    def sent(t, carry):
        hop_right(t // 2, t % 2, RIGHT_HOPS - 1).wait_send()
        hop_left(t // 2, t % 2, LEFT_HOPS - 1).wait_send()
        return carry

    lax.fori_loop(0, 2 * HEADS, sent, 0)
    q_move.wait_send()

    def drain(h):
        for j in range(8):
            c_move(h, j).wait_send()

    def project(h, carry):
        @pl.when(h > 0)
        def _():
            drain(h - 1)

        for j in (2, 1, 3, 6, 5, 7, 4):
            g_move(h, j).wait_recv()
            c_move(h, j).start()
        for j in range(1, 8):
            g_move(h, j).wait_send()
        for move in o_moves(h):
            move.wait_send()
        for j in range(8):
            c_move(h, j).wait_recv()
        part = jnp.dot(wp[h], att[h].reshape(16 * HD, TOK), preferred_element_type=jnp.float32)
        out[...] = out[...] + part
        return carry

    out[...] = jnp.zeros_like(out)
    lax.fori_loop(0, HEADS, project, 0)
    drain(HEADS - 1)


def on_device(queries, fresh_kv, stale_kv, residual, gate, w_out):
    bf16, f32 = jnp.bfloat16, jnp.float32
    in_hbm = pl.BlockSpec(memory_space=pltpu.HBM)
    dma = pltpu.SemaphoreType.DMA
    operands = (queries, fresh_kv.transpose(1, 0, 2), stale_kv.transpose(1, 0, 2), w_out)
    projected = pl.pallas_call(
        fused,
        out_shape=jax.ShapeDtypeStruct((HEADS * HD, TOK), f32),
        in_specs=[in_hbm] * 4,
        out_specs=pl.BlockSpec(memory_space=pltpu.VMEM),
        scratch_shapes=[
            pltpu.VMEM((HEADS, RING, TOK, 2 * HD), bf16),
            pltpu.VMEM((HEADS, TOK, 2 * HD), bf16),
            pltpu.VMEM((HEADS * HD, TOK), bf16),
            pltpu.VMEM((HEADS * HD, TOK), bf16),
            pltpu.VMEM((HEADS * HD, 16 * HEADS * HD), bf16),
            pltpu.VMEM((HEADS, HEADS * HD, 16 * HD), bf16),
            pltpu.VMEM((HEADS, 2 * HD, 2 * TOK), bf16),
            pltpu.VMEM((HEADS, ROWS, 2 * TOK), f32),
            pltpu.VMEM((HEADS, 1, 2 * TOK), f32),
            pltpu.VMEM((HEADS, HD, TOK), bf16),
            pltpu.VMEM((HEADS, 2, TOK), f32),
            pltpu.VMEM((HEADS, HD, TOK), bf16),
            pltpu.VMEM((HEADS, 2, TOK), f32),
            pltpu.VMEM((HEADS, 16, HD, TOK), bf16),
            dma((4,)),
            dma((2, HEADS, 2, LEFT_HOPS)),
            dma((2, HEADS, 2, LEFT_HOPS)),
            dma((7,)),
            dma((7,)),
            dma((HEADS, 8)),
            dma((HEADS, 8)),
            dma((HEADS, 8)),
            dma((HEADS, 8)),
        ],
        compiler_params=pltpu.CompilerParams(
            collective_id=0, has_side_effects=True, vmem_limit_bytes=40 * 1024 * 1024),
        cost_estimate=pl.CostEstimate(
            flops=2_000_000_000, bytes_accessed=4_000_000, transcendentals=6_500_000),
    )(*[pltpu.with_memory_space_constraint(operand, pltpu.HBM) for operand in operands])
    result = residual.astype(f32) + gate[:, None] * projected
    return result.astype(bf16)


def solution(mesh):
    placed = (
        P("head", "patch"),
        P("patch", "head", None),
        P("patch", "head", None),
        P("head", "patch"),
        P("head"),
        P("head", None),
    )
    return jax.shard_map(
        on_device, mesh=mesh, in_specs=placed, out_specs=P("head", "patch"), check_vma=False
    )
```
